256 devices in a mesh: dp: 32 (over z, x), mp: 8 (over y, core).
Axes of the slice: x: 4, y: 4, z: 8, core: 2. Of those that a mesh axis runs over, the one named last changes fastest.
Arguments:
- gradient: bfloat16 [4, 8192, 8192], P(None, 'dp', 'mp')
- owners: int32 [256], replicated, may hold values from 0 to 31, as said below
- left_basis: bfloat16 [256, 1024, 1024], P(('dp', 'mp')), may hold values from -0.1875 to 0.1875
- right_basis: bfloat16 [256, 1024, 1024], P(('dp', 'mp')), may hold values from -0.1875 to 0.1875
- first_moment: bfloat16 [256, 1024, 1024], P(('dp', 'mp')), may hold values from -0.1796875 to 0.1796875
- second_moment: bfloat16 [256, 1024, 1024], P(('dp', 'mp')), may hold values from 1.9907951e-05 to 0.00019931793
Outputs:
- update: bfloat16 [4, 8192, 8192], P(None, 'dp', 'mp')
The draws below stay inside these ranges and needn't reach their ends.
Inputs may be any that keep to these rules, and one draw needn't show every extreme that they name: owners[t] is the data index of the device that owns tile t, whose model index is t mod 8; the tiles of one model index have distinct owners.
All inputs are finite; a program needn't handle non-finite values.
Results may differ from the reference program's by a relative error of at most 0.019.
Values may be sent and summed in bfloat16 or wider, within the bound.
A program may use at most 64 MiB of HBM per device.

```python
import math
import jax
import jax.numpy as jnp
from jax import lax

BLOCK = 1024
QUARTERS = 4
TILES = 256
N_DP = 32
N_MP = 8


def draw_gradient(key, part):
    key = jax.random.fold_in(key, 11)
    subkeys = jax.random.split(key, 3)
    row_total = N_DP * BLOCK // QUARTERS
    col_total = N_MP * BLOCK
    row_position = jnp.arange(row_total, dtype=jnp.float32) / row_total
    col_position = jnp.arange(col_total, dtype=jnp.float32) / col_total
    spread = math.log(10.0 / 3.0)
    trend_power = 0.5
    values_drawn = jax.random.normal(subkeys[0], (QUARTERS, row_total, col_total), jnp.float32)
    row_scale = jnp.exp(jax.random.uniform(subkeys[1], (QUARTERS, row_total, 1), jnp.float32, 0.0, spread))
    row_scale = row_scale * (3.0 ** (trend_power * row_position))[None, :, None]
    col_scale = jnp.exp(jax.random.uniform(subkeys[2], (QUARTERS, 1, col_total), jnp.float32, 0.0, spread))
    col_scale = col_scale * (3.0 ** (trend_power * col_position))[None, None, :]
    return (values_drawn * row_scale * col_scale).astype(jnp.bfloat16)


def draw_owners(key, part):
    key = jax.random.fold_in(key, 23)
    column_keys = jax.random.split(key, N_MP)
    orders = jax.vmap(lambda single: jax.random.permutation(single, N_DP))(column_keys)
    return orders.astype(jnp.int32).T.reshape(TILES)


def block_levels(stream_key, shape, shards, low, largest):
    gain = 1.0
    for dim, blocks in shards:
        draws = jax.random.uniform(jax.random.fold_in(jax.random.fold_in(stream_key, 6), dim), (blocks,), jnp.float32, low / len(shards), largest / len(shards))
        gain = gain * jnp.repeat(jnp.exp(draws), shape[dim] // blocks).reshape((-1,) + (1,) * (len(shape) - 1 - dim))
    return gain


def centred(own_key, extent, scale, bound, pieces=(), kind=jnp.bfloat16):
    result = scale * jax.random.normal(own_key, extent, jnp.float32)
    if pieces:
        result = result * block_levels(own_key, extent, pieces, -0.22, 0.18)
    return jnp.clip(result, -bound, bound).astype(kind)


def setup_inputs(seed: int = 0) -> dict:
    key_of = jax.random.split(jax.random.key(seed), 7)
    gradient = draw_gradient(jax.random.fold_in(key_of[6], 71), 0)
    owners = draw_owners(jax.random.fold_in(key_of[6], 71), 0)
    left_basis = centred(key_of[2], (TILES, BLOCK, BLOCK), BLOCK ** -0.5, 0.1875, ((0, 256),))
    right_basis = centred(key_of[3], (TILES, BLOCK, BLOCK), BLOCK ** -0.5, 0.1875, ((0, 256),))
    first_moment = centred(key_of[4], (TILES, BLOCK, BLOCK), 0.03, 0.1796875, ((0, 256),))
    second_moment = jnp.clip(jnp.exp(math.log(0.00019931793) - 2.303782 * jax.random.uniform(key_of[5], (TILES, BLOCK, BLOCK), jnp.float32) ** block_levels(key_of[5], (TILES, BLOCK, BLOCK), ((0, 256),), -0.2, 0.2)), 1.990795135498047e-05, 0.00019931793).astype(jnp.bfloat16)
    return {"gradient": gradient, "owners": owners, "left_basis": left_basis, "right_basis": right_basis, "first_moment": first_moment, "second_moment": second_moment}


beta_one = 0.9
beta_two = 0.999
epsilon = 1e-08
correct_one = 1.0 - 0.9 ** 3
correct_two = 1.0 - 0.999 ** 3
clip_rms = 0.25

def precondition(grad_tile, left_tile, right_tile, first_tile, second_tile, factor):
    rotated = lax.dot_general(left_tile, grad_tile, (((0,), (0,)), ((), ())), preferred_element_type=jnp.float32)
    rotated = rotated.astype(jnp.bfloat16)
    turned = jnp.dot(rotated, right_tile, preferred_element_type=jnp.float32) * factor
    first_new = beta_one * first_tile.astype(jnp.float32) + (1.0 - beta_one) * turned
    second_new = beta_two * second_tile.astype(jnp.float32) + (1.0 - beta_two) * turned * turned
    step_rotated = (first_new / correct_one / (jnp.sqrt(second_new / correct_two) + epsilon)).astype(jnp.bfloat16)
    back_columns = lax.dot_general(step_rotated, right_tile, (((1,), (1,)), ((), ())), preferred_element_type=jnp.float32)
    back_columns = back_columns.astype(jnp.bfloat16)
    return jnp.dot(left_tile, back_columns, preferred_element_type=jnp.float32).astype(jnp.bfloat16)

def reference(gradient, owners, left_basis, right_basis, first_moment, second_moment):
    groups = N_DP // QUARTERS

    def view_squares(view):
        return jnp.sum(jnp.square(view.astype(jnp.float32)))
    total_squares = jnp.sum(lax.map(view_squares, gradient))
    clip_limit = clip_rms * math.sqrt(TILES * BLOCK * BLOCK)
    factor = jnp.minimum(jnp.float32(1.0), clip_limit / jnp.sqrt(total_squares))

    def one_tile(tile_index):
        row_group = tile_index // N_MP
        column = tile_index % N_MP
        stack = row_group // groups
        block_row = row_group % groups
        zero = jnp.zeros((), jnp.int32)
        grad_tile = lax.dynamic_slice(gradient, (stack.astype(jnp.int32), (block_row * BLOCK).astype(jnp.int32), (column * BLOCK).astype(jnp.int32)), (1, BLOCK, BLOCK))[0]
        owner_slot = (owners[tile_index] * N_MP + column).astype(jnp.int32)
        return precondition(grad_tile, left_basis[owner_slot], right_basis[owner_slot], first_moment[owner_slot], second_moment[owner_slot], factor)
    tiles = lax.map(one_tile, jnp.arange(TILES, dtype=jnp.int32))
    tiles = tiles.reshape(QUARTERS, groups, N_MP, BLOCK, BLOCK).transpose(0, 1, 3, 2, 4)
    return tiles.reshape(QUARTERS, groups * BLOCK, N_MP * BLOCK)
```

```python
import functools
import math

import jax
import jax.numpy as jnp
from jax import lax
from jax.experimental import pallas as pl
from jax.experimental.pallas import tpu as pltpu
from jax.sharding import PartitionSpec as P

MESH = pl.DeviceIdType.MESH
B = 1024
S = 4
NZ, NX, NM = 8, 4, 8
ND = NZ * NX
Q = B // NX
H = Q // NZ
C = 4
W = B // C
T = 256

beta_one = 0.9
beta_two = 0.999
epsilon = 1e-08
correct_one = 1.0 - 0.9**3
correct_two = 1.0 - 0.999**3
clip_limit = 0.25 * math.sqrt(ND * NM * B * B)


def await_bytes(ref, sem):
    pltpu.make_async_copy(ref, ref, sem).wait()


def kernel(grad, owners, left, right, first, second, out,
           gbuf, lv, lt, rv, m1v, m2v, send2, tile, rot, turned, step, back, send3, send4, landed,
           inverse, part, part_z, part_x, part_m,
           s1s, s1r, s2s, s2r, s3s, s3r, s4s, s4r, pss, psr, loc, *arrivals):
    recv1, recv3 = arrivals[:C], arrivals[C:]
    d = lax.axis_index("dp")
    m = lax.axis_index("mp")
    z, x = d // NX, d % NX

    barrier = pltpu.get_barrier_semaphore()

    def greet(i, _):
        pl.semaphore_signal(barrier, inc=1, device_id=((d + i) % ND, m), device_id_type=MESH)
        return 0

    def greet_m(i, _):
        pl.semaphore_signal(barrier, inc=1, device_id=(d, (m + i) % NM), device_id_type=MESH)
        return 0

    local = [
        pltpu.make_async_copy(grad, gbuf, loc.at[0]),
        pltpu.make_async_copy(left.at[0], lv, loc.at[1]),
        pltpu.make_async_copy(right.at[0], rv, loc.at[2]),
        pltpu.make_async_copy(first.at[0], m1v, loc.at[3]),
        pltpu.make_async_copy(second.at[0], m2v, loc.at[4]),
    ]
    lax.fori_loop(1, ND, greet, 0)
    lax.fori_loop(1, NM, greet_m, 0)
    for copy in local:
        copy.start()
    pl.semaphore_wait(barrier, ND - 1 + NM - 1)

    def cols(k):
        return pl.ds(pl.multiple_of(k * W, W), W)

    def spread(k, i, _):
        to = (z + (i * 3) % NZ) % NZ
        pltpu.make_async_remote_copy(
            src_ref=grad.at[:, pl.ds(pl.multiple_of(to * H, H), H), cols(k)],
            dst_ref=recv1[k].at[pl.ds(z * S, S)],
            send_sem=s1s.at[k],
            recv_sem=s1r.at[k],
            device_id=(to * NX + x, m),
            device_id_type=MESH,
        ).start()
        return 0

    for k in range(C):
        lax.fori_loop(1, NZ, functools.partial(spread, k), 0)

    local[0].wait()

    def squares(i, acc):
        block = gbuf[i // 16, pl.ds(pl.multiple_of((i % 16) * 16, 16), 16), :].astype(jnp.float32)
        return acc + block * block

    acc = lax.fori_loop(0, 64, squares, jnp.zeros((16, B), jnp.float32))
    acc = acc[:8] + acc[8:]
    total = acc[:, :128]
    for i in range(1, 8):
        total = total + acc[:, i * 128 : (i + 1) * 128]
    part[0] = total
    part_z[z] = total

    def tell_z(i, _):
        to = (z + i) % NZ
        pltpu.make_async_remote_copy(
            src_ref=part.at[0], dst_ref=part_z.at[z], send_sem=pss.at[0], recv_sem=psr.at[0],
            device_id=(to * NX + x, m), device_id_type=MESH,
        ).start()
        return 0

    lax.fori_loop(1, NZ, tell_z, 0)

    def invert(o, _):
        found = jnp.int32(0)
        for j in range(ND):
            found = found + jnp.where(owners[j * NM + m] == o, (j % NZ) * S + j // NZ, 0)
        inverse[o] = jnp.minimum(found, ND - 1)
        return 0

    lax.fori_loop(0, ND, invert, 0)

    local[1].wait()

    def turn(i, _):
        rows = pl.ds(pl.multiple_of(i * T, T), T)
        lt[:, rows] = lv[rows, :].T
        return 0

    lax.fori_loop(0, B // T, turn, 0)

    def forward(k):
        for s in range(S):
            recv1[k][z * S + s] = gbuf[s, pl.ds(pl.multiple_of(z * H, H), H), cols(k)]
        await_bytes(recv1[k].at[pl.ds(0, 7 * S)], s1r.at[k])

        def send(i, _):
            o = ((z + ((i // NX) * 3) % NZ) % NZ) * NX + (x + i % NX) % NX
            send2[k, o] = recv1[k][inverse[o]]
            pltpu.make_async_remote_copy(
                src_ref=send2.at[k, o],
                dst_ref=tile.at[k, pl.ds(pl.multiple_of(x * Q + z * H, H), H), :],
                send_sem=s2s.at[k],
                recv_sem=s2r.at[k],
                device_id=(o, m),
                device_id_type=MESH,
            ).start()
            return 0

        lax.fori_loop(1, ND, send, 0)
        tile[k, pl.ds(pl.multiple_of(x * Q + z * H, H), H), :] = recv1[k][inverse[d]]

    for k in range(C):
        forward(k)

    await_bytes(part_z.at[pl.ds(0, 7)], psr.at[0])
    total = part_z[0]
    for i in range(1, NZ):
        total = total + part_z[i]
    part[1] = total
    part_x[x] = total

    def tell_x(i, _):
        pltpu.make_async_remote_copy(
            src_ref=part.at[1], dst_ref=part_x.at[x], send_sem=pss.at[1], recv_sem=psr.at[1],
            device_id=(z * NX + (x + i) % NX, m), device_id_type=MESH,
        ).start()
        return 0

    lax.fori_loop(1, NX, tell_x, 0)

    def clear(i, _):
        turned[pl.ds(pl.multiple_of(i * T, T), T), :] = jnp.zeros((T, B), jnp.float32)
        return 0

    lax.fori_loop(0, B // T, clear, 0)
    local[2].wait()

    def rotate(k, _):
        await_bytes(tile.at[k, pl.ds(0, 31 * H), :], s2r.at[k])

        def rows_of(i, _):
            rows = pl.ds(pl.multiple_of(i * T, T), T)
            rot[...] = jnp.dot(lt[rows, :], tile[k], preferred_element_type=jnp.float32).astype(jnp.bfloat16)
            turned[rows, :] += jnp.dot(rot[...], rv[cols(k), :], preferred_element_type=jnp.float32)
            return 0

        lax.fori_loop(0, B // T, rows_of, 0)
        return 0

    lax.fori_loop(0, 1, rotate, 0)
    await_bytes(part_x.at[pl.ds(0, 3)], psr.at[1])
    total = part_x[0]
    for i in range(1, NX):
        total = total + part_x[i]
    part[2] = total
    part_m[m] = total

    def tell_m(i, _):
        pltpu.make_async_remote_copy(
            src_ref=part.at[2], dst_ref=part_m.at[m], send_sem=pss.at[2], recv_sem=psr.at[2],
            device_id=(d, (m + i) % NM), device_id_type=MESH,
        ).start()
        return 0

    lax.fori_loop(1, NM, tell_m, 0)
    lax.fori_loop(1, C, rotate, 0)
    await_bytes(part_m.at[pl.ds(0, 7)], psr.at[2])
    total = part_m[0]
    for i in range(1, NM):
        total = total + part_m[i]
    total_squares = jnp.sum(total, keepdims=True)
    factor = jnp.minimum(jnp.float32(1.0), clip_limit / jnp.sqrt(total_squares))
    local[3].wait()
    local[4].wait()

    def precondition(i, _):
        rows = pl.ds(pl.multiple_of(i * 32, 32), 32)
        t = turned[rows, :] * factor
        first_new = beta_one * m1v[rows, :].astype(jnp.float32) + (1.0 - beta_one) * t
        second_new = beta_two * m2v[rows, :].astype(jnp.float32) + (1.0 - beta_two) * t * t
        value = first_new * (1.0 / correct_one) / (jnp.sqrt(second_new * (1.0 / correct_two)) + epsilon)
        step[rows, :] = value.astype(jnp.bfloat16)
        return 0

    lax.fori_loop(0, B // 32, precondition, 0)

    def produce(k):
        def columns_of(i, _):
            rows = pl.ds(pl.multiple_of(i * T, T), T)
            back[rows, :] = lax.dot_general(
                step[rows, :], rv[cols(k), :], (((1,), (1,)), ((), ())), preferred_element_type=jnp.float32
            ).astype(jnp.bfloat16)
            return 0

        lax.fori_loop(0, B // T, columns_of, 0)

        def rows_of(i, _):
            rows = pl.ds(pl.multiple_of(i * T, T), T)
            send3[k, rows, :] = jnp.dot(lv[rows, :], back[...], preferred_element_type=jnp.float32).astype(jnp.bfloat16)
            return 0

        lax.fori_loop(0, B // T, rows_of, 0)

        def send(i, _):
            zz, xx = (z + ((i // NX) * 3) % NZ) % NZ, (x + i % NX) % NX
            pltpu.make_async_remote_copy(
                src_ref=send3.at[k, pl.ds(pl.multiple_of(xx * Q + zz * H, H), H), :],
                dst_ref=recv3[k].at[d],
                send_sem=s3s.at[k],
                recv_sem=s3r.at[k],
                device_id=(zz * NX + xx, m),
                device_id_type=MESH,
            ).start()
            return 0

        lax.fori_loop(1, ND, send, 0)
        recv3[k][d] = send3[k, pl.ds(pl.multiple_of(x * Q + z * H, H), H), :]

    for k in range(C):
        produce(k)

    def collect(k):
        await_bytes(recv3[k].at[pl.ds(0, 31)], s3r.at[k])

        def send(i, _):
            to = (z + (i * 3) % NZ) % NZ
            for s in range(S):
                send4[k, to, s] = recv3[k][owners[(s * NZ + to) * NM + m]]
            pltpu.make_async_remote_copy(
                src_ref=send4.at[k, to],
                dst_ref=landed.at[:, pl.ds(pl.multiple_of(z * H, H), H), cols(k)],
                send_sem=s4s.at[k],
                recv_sem=s4r.at[k],
                device_id=(to * NX + x, m),
                device_id_type=MESH,
            ).start()
            return 0

        lax.fori_loop(1, NZ, send, 0)
        for s in range(S):
            landed[s, pl.ds(pl.multiple_of(z * H, H), H), cols(k)] = recv3[k][owners[(s * NZ + z) * NM + m]]

    for k in range(C):
        collect(k)

    def finish(k, _):
        await_bytes(send4.at[k, pl.ds(0, 7)], s4r.at[k])
        pltpu.make_async_copy(landed.at[:, :, cols(k)], out.at[:, :, cols(k)], loc.at[5]).start()
        return 0

    lax.fori_loop(0, C, finish, 0)

    def drain(k, _):
        await_bytes(send4.at[k, pl.ds(0, 7)], s1s.at[k])
        await_bytes(send2.at[k, pl.ds(0, 31)], s2s.at[k])
        await_bytes(send2.at[k, pl.ds(0, 31)], s3s.at[k])
        await_bytes(send4.at[k, pl.ds(0, 7)], s4s.at[k])
        return 0

    lax.fori_loop(0, C, drain, 0)
    await_bytes(part_z.at[pl.ds(0, 7)], pss.at[0])
    await_bytes(part_x.at[pl.ds(0, 3)], pss.at[1])
    await_bytes(part_m.at[pl.ds(0, 7)], pss.at[2])
    await_bytes(landed, loc.at[5])


def per_device(*args):
    bf16, f32 = jnp.bfloat16, jnp.float32
    whole = pl.BlockSpec(memory_space=pl.ANY)
    dma = pltpu.SemaphoreType.DMA
    return pl.pallas_call(
        kernel,
        out_shape=jax.ShapeDtypeStruct((S, Q, B), bf16),
        in_specs=[whole, pl.BlockSpec(memory_space=pltpu.SMEM), whole, whole, whole, whole],
        out_specs=whole,
        scratch_shapes=[
            pltpu.VMEM((S, Q, B), bf16),
            pltpu.VMEM((B, B), bf16),
            pltpu.VMEM((B, B), bf16),
            pltpu.VMEM((B, B), bf16),
            pltpu.VMEM((B, B), bf16),
            pltpu.VMEM((B, B), bf16),
            pltpu.VMEM((C, ND, H, W), bf16),
            pltpu.VMEM((C, B, W), bf16),
            pltpu.VMEM((T, W), bf16),
            pltpu.VMEM((B, B), f32),
            pltpu.VMEM((B, B), bf16),
            pltpu.VMEM((B, W), bf16),
            pltpu.VMEM((C, B, W), bf16),
            pltpu.VMEM((C, NZ, S, H, W), bf16),
            pltpu.VMEM((S, Q, B), bf16),
            pltpu.SMEM((ND,), jnp.int32),
            pltpu.VMEM((3, 8, 128), f32),
            pltpu.VMEM((NZ, 8, 128), f32),
            pltpu.VMEM((NX, 8, 128), f32),
            pltpu.VMEM((NM, 8, 128), f32),
        ]
        + [dma((C,))] * 8
        + [dma((3,)), dma((3,)), dma((6,))]
        + [pltpu.VMEM((ND, H, W), bf16)] * (2 * C),
        compiler_params=pltpu.CompilerParams(collective_id=0, has_side_effects=True, vmem_limit_bytes=56 << 20),
        cost_estimate=pl.CostEstimate(flops=8 * B**3, bytes_accessed=14 * B * B, transcendentals=2 * B * B),
        name="soap_step",
    )(*args)


def solution(mesh):
    placed = (
        P(None, "dp", "mp"),
        P(),
        P(("dp", "mp"), None, None),
        P(("dp", "mp"), None, None),
        P(("dp", "mp"), None, None),
        P(("dp", "mp"), None, None),
    )
    return jax.shard_map(
        per_device, mesh=mesh, in_specs=placed, out_specs=P(None, "dp", "mp"), check_vma=False
    )
```

```python
import math

import jax
import jax.numpy as jnp
from jax import lax
from jax.experimental import pallas as pl
from jax.experimental.pallas import tpu as pltpu
from jax.sharding import PartitionSpec as P

MESH = pl.DeviceIdType.MESH
B = 1024
S = 4
NZ, NX, NM = 8, 4, 8
ND = NZ * NX
Q = B // NX
H = Q // NZ
C = 4
W = B // C
T = 256
R = NX * H

beta_one = 0.9
beta_two = 0.999
epsilon = 1e-08
correct_one = 1.0 - 0.9**3
correct_two = 1.0 - 0.999**3
clip_limit = 0.25 * math.sqrt(ND * NM * B * B)


def await_bytes(ref, sem):
    pltpu.make_async_copy(ref, ref, sem).wait()


def send(src, dst, send_sem, recv_sem, to):
    pltpu.make_async_remote_copy(
        src_ref=src, dst_ref=dst, send_sem=send_sem, recv_sem=recv_sem, device_id=to, device_id_type=MESH
    ).start()


class Ring:
    def __init__(self, source, deliver, spread, refs):
        self.source, self.deliver, self.spread = source, deliver, spread
        self.t1, self.t2, self.t3, self.ss, self.st, self.sf = refs
        d, self.m = lax.axis_index("dp"), lax.axis_index("mp")
        self.z, self.x = d // NX, d % NX

    def ways(self):
        for i, way in ((0, 1), (1, NZ - 1)):
            yield i, way, (((self.z + way) % NZ) * NX + self.x, self.m)

    def off(self, n):
        return (self.z + n) % NZ

    def land(self, piece, k, origin, way, hop, part):
        sem = self.sf.at[hop if self.spread == "hop" else k]
        zz = self.off(way)
        if not self.spread:
            send(piece(part), self.deliver(k, origin, part), self.ss.at[3, k], sem, (zz * NX + self.x, self.m))
            return
        for n in range(part.size):
            j = part.start + (self.x + n) % part.size
            send(piece(pl.ds(j, 1)), self.deliver(k, origin), self.ss.at[3, k], sem, (zz * NX + j, self.m))

    def hop1(self, k, planes=(4, 3, 2, 1)):
        for i, way, to in self.ways():
            for n, place in ((4, pl.ds(0, 2)), (3, pl.ds(2, 4)), (2, pl.ds(6, 4))):
                if n in planes:
                    zz, part = (self.off(4), pl.ds(2 * i, 2)) if n == 4 else (self.off(n * way), ALL)
                    send(self.source(k, zz, part), self.t1.at[i, k, place], self.ss.at[0, k], self.st.at[i, 0, k], to)
            if 1 in planes:
                self.land(lambda p: self.source(k, self.off(way), p), k, self.z, way, 1, ALL)

    def hop2(self, k):
        for i, way, to in self.ways():
            await_bytes(self.t1.at[i, k], self.st.at[i, 0, k])
            send(self.t1.at[i, k, pl.ds(0, 6)], self.t2.at[i, k], self.ss.at[1, k], self.st.at[i, 1, k], to)
            self.land(lambda p: self.t1.at[i, k, pl.ds(6 + p.start, p.size)], k, self.off(NZ - way), way, 2, ALL)

    def hop3(self, k):
        for i, way, to in self.ways():
            await_bytes(self.t2.at[i, k], self.st.at[i, 1, k])
            send(self.t2.at[i, k, pl.ds(0, 2)], self.t3.at[i, k], self.ss.at[2, k], self.st.at[i, 2, k], to)
            self.land(lambda p: self.t2.at[i, k, pl.ds(2 + p.start, p.size)], k, self.off(2 * (NZ - way)), way, 3, ALL)

    def hop4(self, k):
        for i, way, to in self.ways():
            await_bytes(self.t3.at[i, k], self.st.at[i, 2, k])
            self.land(
                lambda p: self.t3.at[i, k, pl.ds(p.start - 2 * i, p.size)],
                k, self.off(3 * (NZ - way)), way, 4, pl.ds(2 * i, 2))

    def along_x(self, k):
        for i in range(1, NX):
            xx = (self.x + i) % NX
            send(self.source(k, self.z, pl.ds(xx, 1)), self.deliver(k, self.z), self.ss.at[3, k],
                 self.sf.at[0 if self.spread == "hop" else k], (self.z * NX + xx, self.m))

    def drain(self, k, whole):
        await_bytes(self.t1.at[:, k], self.ss.at[0, k])
        await_bytes(self.t2.at[:, k], self.ss.at[1, k])
        await_bytes(self.t3.at[:, k], self.ss.at[2, k])
        await_bytes(whole.at[pl.ds(0, 31 if self.spread else 28)], self.ss.at[3, k])


ALL = pl.ds(0, 4)


def cols(k):
    return pl.ds(k * W, W)


def rows_of_plane(zz):
    return pl.ds(pl.multiple_of(zz * H, H), H)


def kernel(grad, owners, left, right, first, second, out,
           gbuf, lv, lt, rv, m1v, m2v, send2, tile, half, turned, step, send3, send4,
           inverse, part, part_z, part_x, part_m, pss, psr, loc, *more):
    recv1, recv3, more = more[:C], more[C : 2 * C], more[2 * C :]
    d = lax.axis_index("dp")
    m = lax.axis_index("mp")
    z, x = d // NX, d % NX

    ring1 = Ring(
        lambda k, zz, part: gbuf.at[part, rows_of_plane(zz), cols(k)],
        lambda k, zz, part: recv1[k].at[pl.ds(zz * S + part.start, part.size)],
        None, more[0:6])
    ring2 = Ring(
        lambda k, zz, part: send2.at[k, pl.ds(zz * NX + part.start, part.size)],
        lambda k, zz: tile.at[zz, pl.ds(x, 1), :, cols(k)],
        "hop", more[6:12])
    ring3 = Ring(
        lambda k, zz, part: send3.at[zz, part, :, cols(k)],
        lambda k, zz: recv3[k].at[pl.ds(zz * NX + x, 1)],
        "chunk", more[12:18])
    ring4 = Ring(
        lambda k, zz, part: send4.at[k, zz, part],
        lambda k, zz, part: out.at[part, rows_of_plane(zz), cols(k)],
        None, more[18:24])

    barrier = pltpu.get_barrier_semaphore()

    def along_z(i):
        return (((z + i) % NZ) * NX + x, m)

    def along_x(i):
        return (z * NX + (x + i) % NX, m)

    def along_m(i):
        return (d, (m + i) % NM)

    local = [
        pltpu.make_async_copy(grad, gbuf, loc.at[0]),
        pltpu.make_async_copy(right.at[0], rv, loc.at[2]),
        pltpu.make_async_copy(first.at[0], m1v, loc.at[3]),
        pltpu.make_async_copy(second.at[0], m2v, loc.at[4]),
    ]
    local[0].start()

    met = [along_z(i) for i in range(1, NZ)] + [along_x(i) for i in range(1, NX)] + [along_m(i) for i in range(1, NM)]
    met += [(((z + way) % NZ) * NX + (x + i) % NX, m) for way in (1, NZ - 1) for i in range(1, NX)]
    for other in met:
        pl.semaphore_signal(barrier, inc=1, device_id=other, device_id_type=MESH)
    local[0].wait()
    pl.semaphore_wait(barrier, len(met))

    def gather_sum(n, value, held, place, axis, size):
        part[n] = value
        held[place] = value
        for i in range(1, size):
            send(part.at[n], held.at[place], pss.at[n], psr.at[n], axis(i))

    def sum_of(n, held, size):
        await_bytes(held.at[pl.ds(0, size - 1)], psr.at[n])
        total = held[0]
        for i in range(1, size):
            total = total + held[i]
        return total

    def squares():
        def add(i, acc):
            block = gbuf[i // 16, pl.ds(pl.multiple_of((i % 16) * 16, 16), 16), :].astype(jnp.float32)
            return acc + block * block

        acc = lax.fori_loop(0, 64, add, jnp.zeros((16, B), jnp.float32))
        acc = acc[:8] + acc[8:]
        total = acc[:, :128]
        for i in range(1, 8):
            total = total + acc[:, i * 128 : (i + 1) * 128]
        gather_sum(0, total, part_z, z, along_z, NZ)

    def invert(low, high):
        def one(o, _):
            found = jnp.int32(0)
            for j in range(ND):
                found = found + jnp.where(owners[j * NM + m] == o, (j % NZ) * S + j // NZ, 0)
            inverse[o] = jnp.minimum(found, ND - 1)
            return 0

        lax.fori_loop(low, high, one, 0)

    def fetch():
        def one(i, _):
            rows = pl.ds(pl.multiple_of((i % NX) * Q + (i // NX) * H, H), H)
            pltpu.make_async_copy(left.at[0, rows, :], lv.at[i // NX, i % NX], loc.at[1]).start()
            return 0

        lax.fori_loop(0, ND, one, 0)
        for copy in local[1:]:
            copy.start()

    def lanes(zz):
        return pl.ds(pl.multiple_of(zz * R, R), R)

    def turn():
        await_bytes(lv, loc.at[1])

        def one(zz, _):
            lt[:, lanes(zz)] = lv[zz].reshape(R, B).T
            turned[lanes(zz), :] = jnp.zeros((R, B), jnp.float32)
            return 0

        lax.fori_loop(0, NZ, one, 0)

    def pack(k):
        for s in range(S):
            recv1[k][z * S + s] = gbuf[s, rows_of_plane(z), cols(k)]
        await_bytes(recv1[k].at[pl.ds(0, 28)], ring1.sf.at[k])

        def one(o, _):
            send2[k, o] = recv1[k][inverse[o]]
            return 0

        lax.fori_loop(0, ND, one, 0, unroll=4)

    def rows_by(ref, planes):
        return jnp.concatenate([ref[zz].reshape(R, B) for zz in planes], axis=0)

    def rotate(*shifts):
        planes = [(z + n) % NZ for n in shifts]
        size = R * len(planes)

        def columns_of(i, _):
            wide = pl.ds(pl.multiple_of(i * T, T), T)
            half[:size, wide] = jnp.dot(
                rows_by(tile, planes), rv[:, wide], preferred_element_type=jnp.float32
            ).astype(jnp.bfloat16)
            return 0

        lax.fori_loop(0, B // T, columns_of, 0)

        def rows_of(i, _):
            rows = pl.ds(pl.multiple_of(i * T, T), T)
            basis = jnp.concatenate([lt[rows, lanes(zz)] for zz in planes], axis=1)
            turned[rows, :] += jnp.dot(basis, half[:size], preferred_element_type=jnp.float32)
            return 0

        lax.fori_loop(0, B // T, rows_of, 0)

    for k in range(C):
        ring1.hop1(k)
    squares()
    fetch()

    def onward(k):
        pack(k)
        ring2.hop1(k)
        ring2.along_x(k)
        tile[z, pl.ds(x, 1), :, cols(k)] = send2[k, pl.ds(d, 1)]

    early, late = range(C // 2), range(C // 2, C)

    def run(*steps):
        for step_of, chunks in steps:
            for k in chunks:
                step_of(k)

    run((ring1.hop2, early))
    invert(0, ND // 2)
    run((ring1.hop3, early), (ring1.hop2, late))
    invert(ND // 2, ND)
    turn()
    run((ring1.hop4, early), (ring1.hop3, late), (onward, early), (ring1.hop4, late), (onward, late))
    gather_sum(1, sum_of(0, part_z, NZ), part_x, x, along_x, NX)
    for k in range(C):
        ring2.hop2(k)
    local[1].wait()
    await_bytes(tile.at[0, pl.ds(0, NX - 1)], ring2.sf.at[0])
    rotate(0)
    gather_sum(2, sum_of(1, part_x, NX), part_m, m, along_m, NM)
    for k in range(C):
        ring2.hop3(k)
    await_bytes(tile.at[pl.ds(0, 2)], ring2.sf.at[1])
    rotate(1, 7)
    for k in range(C):
        ring2.hop4(k)
    await_bytes(tile.at[pl.ds(0, 2)], ring2.sf.at[2])
    rotate(2, 6)
    await_bytes(tile.at[pl.ds(0, 2)], ring2.sf.at[3])
    rotate(3, 5)
    await_bytes(tile.at[0], ring2.sf.at[4])
    rotate(4)

    total_squares = jnp.sum(sum_of(2, part_m, NM), keepdims=True)
    factor = jnp.minimum(jnp.float32(1.0), clip_limit / jnp.sqrt(total_squares))
    local[2].wait()
    local[3].wait()

    def precondition(i, _):
        rows = pl.ds(pl.multiple_of(i * 32, 32), 32)
        t = turned[rows, :] * factor
        first_new = (beta_one / correct_one) * m1v[rows, :].astype(jnp.float32) + ((1.0 - beta_one) / correct_one) * t
        second_new = (beta_two / correct_two) * m2v[rows, :].astype(jnp.float32)
        second_new = second_new + ((1.0 - beta_two) / correct_two) * (t * t)
        value = first_new / (second_new * lax.rsqrt(second_new) + epsilon)
        step[rows, :] = value.astype(jnp.bfloat16)
        return 0

    lax.fori_loop(0, B // 32, precondition, 0)

    def produce(*shifts):
        planes = [(z + n) % NZ for n in shifts]
        size = R * len(planes)

        def columns_of(i, _):
            wide = pl.ds(pl.multiple_of(i * T, T), T)
            half[:size, wide] = jnp.dot(
                rows_by(lv, planes), step[:, wide], preferred_element_type=jnp.float32
            ).astype(jnp.bfloat16)
            return 0

        lax.fori_loop(0, B // T, columns_of, 0)

        def back(i, _):
            wide = pl.ds(pl.multiple_of(i * T, T), T)
            value = lax.dot_general(
                half[:size], rv[wide, :], (((1,), (1,)), ((), ())), preferred_element_type=jnp.float32
            ).astype(jnp.bfloat16)
            for n, zz in enumerate(planes):
                send3[zz, :, :, wide] = value[n * R : (n + 1) * R].reshape(NX, H, T)
            return 0

        lax.fori_loop(0, B // T, back, 0)

    for n in (4, 3, 2, 1):
        produce(*sorted({n, NZ - n}))
        for k in range(C):
            ring3.hop1(k, (n,))
    produce(0)
    for k in range(C):
        ring3.along_x(k)
        recv3[k][pl.ds(d, 1)] = send3[z, pl.ds(x, 1), :, cols(k)]

    def place(k):
        await_bytes(recv3[k].at[pl.ds(0, 31)], ring3.sf.at[k])

        def one(zz, _):
            for s in range(S):
                send4[k, zz, s] = recv3[k][owners[(s * NZ + zz) * NM + m]]
            return 0

        lax.fori_loop(0, NZ, one, 0)
        ring4.hop1(k)
        out[:, rows_of_plane(z), cols(k)] = send4[k, z]

    def finish(k):
        await_bytes(send4.at[k, pl.ds(0, 7)], ring4.sf.at[k])

    run((ring3.hop2, early), (ring3.hop3, early), (ring3.hop2, late), (ring3.hop4, early), (ring3.hop3, late))
    run((place, early), (ring3.hop4, late), (place, late))
    run((ring4.hop2, range(C)), (ring4.hop3, range(C)), (ring4.hop4, range(C)), (finish, range(C)))

    for k in range(C):
        for ring in (ring1, ring2, ring3, ring4):
            ring.drain(k, recv1[k])
    await_bytes(part_z.at[pl.ds(0, NZ - 1)], pss.at[0])
    await_bytes(part_x.at[pl.ds(0, NX - 1)], pss.at[1])
    await_bytes(part_m.at[pl.ds(0, NM - 1)], pss.at[2])


def per_device(*args):
    bf16, f32 = jnp.bfloat16, jnp.float32
    whole = pl.BlockSpec(memory_space=pl.ANY)
    dma = pltpu.SemaphoreType.DMA

    def vmem(*shape):
        return pltpu.VMEM(shape, bf16)

    ring = [vmem(2, C, 10, H, W), vmem(2, C, 6, H, W), vmem(2, C, 2, H, W), dma((4, C)), dma((2, 3, C)), dma((max(C, 5),))]
    return pl.pallas_call(
        kernel,
        out_shape=vmem(S, Q, B),
        in_specs=[whole, pl.BlockSpec(memory_space=pltpu.SMEM), whole, whole, whole, whole],
        out_specs=pl.BlockSpec(memory_space=pltpu.VMEM),
        scratch_shapes=[
            vmem(S, Q, B),
            vmem(NZ, NX, H, B),
            vmem(B, B),
            vmem(B, B),
            vmem(B, B),
            vmem(B, B),
            vmem(C, ND, H, W),
            vmem(NZ, NX, H, B),
            vmem(2 * R, B),
            pltpu.VMEM((B, B), f32),
            vmem(B, B),
            vmem(NZ, NX, H, B),
            vmem(C, NZ, S, H, W),
            pltpu.SMEM((ND,), jnp.int32),
            pltpu.VMEM((3, 8, 128), f32),
            pltpu.VMEM((NZ, 8, 128), f32),
            pltpu.VMEM((NX, 8, 128), f32),
            pltpu.VMEM((NM, 8, 128), f32),
            dma((3,)),
            dma((3,)),
            dma((6,)),
        ]
        + [vmem(ND, H, W)] * (2 * C)
        + ring * 4,
        compiler_params=pltpu.CompilerParams(collective_id=0, has_side_effects=True, vmem_limit_bytes=58 << 20),
        cost_estimate=pl.CostEstimate(flops=8 * B**3, bytes_accessed=14 * B * B, transcendentals=2 * B * B),
        name="soap_step",
    )(*args)


def solution(mesh):
    placed = (
        P(None, "dp", "mp"),
        P(),
        P(("dp", "mp"), None, None),
        P(("dp", "mp"), None, None),
        P(("dp", "mp"), None, None),
        P(("dp", "mp"), None, None),
    )
    return jax.shard_map(
        per_device, mesh=mesh, in_specs=placed, out_specs=P(None, "dp", "mp"), check_vma=False
    )
```

```python
import math

import jax
import jax.numpy as jnp
from jax import lax
from jax.experimental import pallas as pl
from jax.experimental.pallas import tpu as pltpu
from jax.sharding import PartitionSpec as P

MESH = pl.DeviceIdType.MESH
B = 1024
S = 4
NZ, NX, NM = 8, 4, 8
ND = NZ * NX
Q = B // NX
H = Q // NZ
C = 4
W = B // C
T = 256
E = 16
R = NX * H

beta_one = 0.9
beta_two = 0.999
epsilon = 1e-08
correct_one = 1.0 - 0.9**3
correct_two = 1.0 - 0.999**3
clip_limit = 0.25 * math.sqrt(ND * NM * B * B)


def await_bytes(ref, sem):
    pltpu.make_async_copy(ref, ref, sem).wait()


def send(src, dst, send_sem, recv_sem, to):
    pltpu.make_async_remote_copy(
        src_ref=src, dst_ref=dst, send_sem=send_sem, recv_sem=recv_sem, device_id=to, device_id_type=MESH
    ).start()


class Ring:
    def __init__(self, source, deliver, spread, refs):
        self.source, self.deliver, self.spread = source, deliver, spread
        self.t1, self.t2, self.t3, self.ss, self.st, self.sf = refs
        d, self.m = lax.axis_index("dp"), lax.axis_index("mp")
        self.z, self.x = d // NX, d % NX

    def ways(self):
        for i, way in ((0, 1), (1, NZ - 1)):
            yield i, way, (((self.z + way) % NZ) * NX + self.x, self.m)

    def off(self, n):
        return (self.z + n) % NZ

    def land(self, piece, k, origin, way, hop, part):
        sem = self.sf.at[hop if self.spread == "hop" else k]
        zz = self.off(way)
        if not self.spread:
            send(piece(part), self.deliver(k, origin, part), self.ss.at[3, k], sem, (zz * NX + self.x, self.m))
            return
        for n in range(part.size):
            j = part.start + (self.x + n) % part.size
            send(piece(pl.ds(j, 1)), self.deliver(k, origin), self.ss.at[3, k], sem, (zz * NX + j, self.m))

    def hop1(self, k, planes=(4, 3, 2, 1)):
        for i, way, to in self.ways():
            for n, place in ((4, pl.ds(0, 2)), (3, pl.ds(2, 4)), (2, pl.ds(6, 4))):
                if n in planes:
                    zz, part = (self.off(4), pl.ds(2 * i, 2)) if n == 4 else (self.off(n * way), ALL)
                    send(self.source(k, zz, part), self.t1.at[i, k, place], self.ss.at[0, k], self.st.at[i, 0, k], to)
            if 1 in planes:
                self.land(lambda p: self.source(k, self.off(way), p), k, self.z, way, 1, ALL)

    def hop2(self, k):
        for i, way, to in self.ways():
            await_bytes(self.t1.at[i, k], self.st.at[i, 0, k])
            send(self.t1.at[i, k, pl.ds(0, 6)], self.t2.at[i, k], self.ss.at[1, k], self.st.at[i, 1, k], to)
            self.land(lambda p: self.t1.at[i, k, pl.ds(6 + p.start, p.size)], k, self.off(NZ - way), way, 2, ALL)

    def hop3(self, k):
        for i, way, to in self.ways():
            await_bytes(self.t2.at[i, k], self.st.at[i, 1, k])
            send(self.t2.at[i, k, pl.ds(0, 2)], self.t3.at[i, k], self.ss.at[2, k], self.st.at[i, 2, k], to)
            self.land(lambda p: self.t2.at[i, k, pl.ds(2 + p.start, p.size)], k, self.off(2 * (NZ - way)), way, 3, ALL)

    def hop4(self, k):
        for i, way, to in self.ways():
            await_bytes(self.t3.at[i, k], self.st.at[i, 2, k])
            self.land(
                lambda p: self.t3.at[i, k, pl.ds(p.start - 2 * i, p.size)],
                k, self.off(3 * (NZ - way)), way, 4, pl.ds(2 * i, 2))

    def along_x(self, k):
        for i in range(1, NX):
            xx = (self.x + i) % NX
            send(self.source(k, self.z, pl.ds(xx, 1)), self.deliver(k, self.z), self.ss.at[3, k],
                 self.sf.at[0 if self.spread == "hop" else k], (self.z * NX + xx, self.m))

    def drain(self, k, whole):
        await_bytes(self.t1.at[:, k], self.ss.at[0, k])
        await_bytes(self.t2.at[:, k], self.ss.at[1, k])
        await_bytes(self.t3.at[:, k], self.ss.at[2, k])
        await_bytes(whole.at[pl.ds(0, 31 if self.spread else 28)], self.ss.at[3, k])


ALL = pl.ds(0, 4)


def cols(k):
    return pl.ds(k * W, W)


def rows_of_plane(zz):
    return pl.ds(pl.multiple_of(zz * H, H), H)


def kernel(grad, owners, left, right, first, second, out,
           gbuf, lv, lt, rv, rt, m1v, m2v, send2, tile, half, rest0, rest1, turned, step, send3, send4,
           inverse, part, part_z, part_x, part_m, pss, psr, loc, *more):
    recv1, recv3, more = more[:C], more[C : 2 * C], more[2 * C :]
    rest = (rest0, rest1)
    d = lax.axis_index("dp")
    m = lax.axis_index("mp")
    z, x = d // NX, d % NX

    ring1 = Ring(
        lambda k, zz, part: gbuf.at[part, rows_of_plane(zz), cols(k)],
        lambda k, zz, part: recv1[k].at[pl.ds(zz * S + part.start, part.size)],
        None, more[0:6])
    ring2 = Ring(
        lambda k, zz, part: send2.at[k, pl.ds(zz * NX + part.start, part.size)],
        lambda k, zz: tile.at[zz, pl.ds(x, 1), :, cols(k)],
        "hop", more[6:12])
    ring3 = Ring(
        lambda k, zz, part: send3.at[zz, part, :, cols(k)],
        lambda k, zz: recv3[k].at[pl.ds(zz * NX + x, 1)],
        "chunk", more[12:18])
    ring4 = Ring(
        lambda k, zz, part: send4.at[k, zz, part],
        lambda k, zz, part: out.at[part, rows_of_plane(zz), cols(k)],
        None, more[18:24])

    barrier = pltpu.get_barrier_semaphore()

    def along_z(i):
        return (((z + i) % NZ) * NX + x, m)

    def along_x(i):
        return (z * NX + (x + i) % NX, m)

    def along_m(i):
        return (d, (m + i) % NM)

    local = [
        pltpu.make_async_copy(grad, gbuf, loc.at[0]),
        pltpu.make_async_copy(right.at[0], rv, loc.at[2]),
        pltpu.make_async_copy(first.at[0], m1v, loc.at[3]),
        pltpu.make_async_copy(second.at[0], m2v, loc.at[4]),
    ]
    local[0].start()

    met = [along_z(i) for i in range(1, NZ)] + [along_x(i) for i in range(1, NX)] + [along_m(i) for i in range(1, NM)]
    met += [(((z + way) % NZ) * NX + (x + i) % NX, m) for way in (1, NZ - 1) for i in range(1, NX)]
    for other in met:
        pl.semaphore_signal(barrier, inc=1, device_id=other, device_id_type=MESH)
    local[0].wait()
    pl.semaphore_wait(barrier, len(met))

    def gather_sum(n, value, held, place, axis, size):
        part[n] = value
        held[place] = value
        for i in range(1, size):
            send(part.at[n], held.at[place], pss.at[n], psr.at[n], axis(i))

    def sum_of(n, held, size):
        await_bytes(held.at[pl.ds(0, size - 1)], psr.at[n])
        total = held[0]
        for i in range(1, size):
            total = total + held[i]
        return total

    def squares():
        def add(i, acc):
            block = gbuf[i // 16, pl.ds(pl.multiple_of((i % 16) * 16, 16), 16), :].astype(jnp.float32)
            return acc + block * block

        acc = lax.fori_loop(0, 64, add, jnp.zeros((16, B), jnp.float32))
        acc = acc[:8] + acc[8:]
        total = acc[:, :128]
        for i in range(1, 8):
            total = total + acc[:, i * 128 : (i + 1) * 128]
        gather_sum(0, total, part_z, z, along_z, NZ)

    def invert(low, high):
        def one(o, _):
            found = jnp.int32(0)
            for j in range(ND):
                found = found + jnp.where(owners[j * NM + m] == o, (j % NZ) * S + j // NZ, 0)
            inverse[o] = jnp.minimum(found, ND - 1)
            return 0

        lax.fori_loop(low, high, one, 0)

    def fetch():
        def one(i, _):
            rows = pl.ds(pl.multiple_of((i % NX) * Q + (i // NX) * H, H), H)
            pltpu.make_async_copy(left.at[0, rows, :], lv.at[i // NX, i % NX], loc.at[1]).start()
            return 0

        lax.fori_loop(0, ND, one, 0)
        for copy in local[1:]:
            copy.start()

    def lanes(zz):
        return pl.ds(pl.multiple_of(zz * R, R), R)

    def turn():
        await_bytes(lv, loc.at[1])

        def one(zz, _):
            lt[:, lanes(zz)] = lv[zz].reshape(R, B).T
            return 0

        lax.fori_loop(0, NZ, one, 0)

    def pack(k):
        for s in range(S):
            recv1[k][z * S + s] = gbuf[s, rows_of_plane(z), cols(k)]
        await_bytes(recv1[k].at[pl.ds(0, 28)], ring1.sf.at[k])

        def one(o, _):
            send2[k, o] = recv1[k][inverse[o]]
            return 0

        lax.fori_loop(0, ND, one, 0, unroll=4)

    def rows_by(ref, planes):
        return jnp.concatenate([ref[zz].reshape(R, B) for zz in planes], axis=0)

    def rotate_rows(at, *shifts):
        planes = [(z + n) % NZ for n in shifts]
        size = R * len(planes)

        def columns_of(i, _):
            wide = pl.ds(pl.multiple_of(i * T, T), T)
            half[at : at + size, wide] = jnp.dot(
                rows_by(tile, planes), rv[:, wide], preferred_element_type=jnp.float32
            ).astype(jnp.bfloat16)
            return 0

        lax.fori_loop(0, B // T, columns_of, 0)

    def left_rows(rows, *shifts):
        basis = jnp.concatenate([lt[rows, lanes((z + n) % NZ)] for n in shifts], axis=1)
        return jnp.dot(basis, half[: R * len(shifts)], preferred_element_type=jnp.float32)

    def rotate(*shifts):
        rotate_rows(0, *shifts)

        def rows_of(i, _):
            rows = pl.ds(pl.multiple_of(i * T, T), T)
            if shifts == (0,):
                turned[rows, :] = left_rows(rows, *shifts)
            else:
                turned[rows, :] += left_rows(rows, *shifts)
            return 0

        lax.fori_loop(0, B // T, rows_of, 0)

    for k in range(C):
        ring1.hop1(k)
    squares()
    fetch()

    def onward(k):
        pack(k)
        ring2.hop1(k)
        ring2.along_x(k)
        tile[z, pl.ds(x, 1), :, cols(k)] = send2[k, pl.ds(d, 1)]

    def run(*steps):
        for step_of, k in steps:
            step_of(k)

    ring1.hop2(0)
    invert(0, ND // 2)
    run((ring1.hop3, 0), (ring1.hop2, 1))
    invert(ND // 2, ND)
    run((ring1.hop4, 0), (ring1.hop3, 1), (ring1.hop2, 2))
    turn()
    run((onward, 0), (ring1.hop4, 1), (ring1.hop3, 2), (ring1.hop2, 3))
    run((onward, 1), (ring1.hop4, 2), (ring1.hop3, 3), (onward, 2), (ring1.hop4, 3), (onward, 3))
    gather_sum(1, sum_of(0, part_z, NZ), part_x, x, along_x, NX)
    for k in range(C):
        ring2.hop2(k)
    local[1].wait()
    await_bytes(tile.at[0, pl.ds(0, NX - 1)], ring2.sf.at[0])
    rotate(0)

    def turn_right(i, _):
        rows = pl.ds(pl.multiple_of(i * T, T), T)
        rt[:, rows] = rv[rows, :].T
        return 0

    lax.fori_loop(0, B // T, turn_right, 0)
    gather_sum(2, sum_of(1, part_x, NX), part_m, m, along_m, NM)
    for k in range(C):
        ring2.hop3(k)
    await_bytes(tile.at[pl.ds(0, 2)], ring2.sf.at[1])
    rotate(1, 7)
    for k in range(C):
        ring2.hop4(k)
    await_bytes(tile.at[pl.ds(0, 2)], ring2.sf.at[2])
    rotate(2, 6)
    await_bytes(tile.at[pl.ds(0, 2)], ring2.sf.at[3])
    rotate_rows(0, 3, 5)
    await_bytes(tile.at[0], ring2.sf.at[4])
    rotate_rows(2 * R, 4)

    total_squares = jnp.sum(sum_of(2, part_m, NM), keepdims=True)
    factor = jnp.minimum(jnp.float32(1.0), clip_limit / jnp.sqrt(total_squares))
    local[2].wait()
    local[3].wait()

    def precondition(i):
        more = rest[i % 2]
        more[...] = left_rows(pl.ds(i * T, T), 3, 5, 4)
        for n in range(0, T, E):
            rows = pl.ds(i * T + n, E)
            t = (turned[rows, :] + more[n : n + E, :]) * factor
            first_new = (beta_one / correct_one) * m1v[rows, :].astype(jnp.float32)
            first_new = first_new + ((1.0 - beta_one) / correct_one) * t
            second_new = (beta_two / correct_two) * m2v[rows, :].astype(jnp.float32)
            second_new = second_new + ((1.0 - beta_two) / correct_two) * (t * t)
            value = first_new / (second_new * lax.rsqrt(second_new) + epsilon)
            step[rows, :] = value.astype(jnp.bfloat16)

    for i in range(B // T):
        precondition(i)

    def produce(*shifts):
        planes = [(z + n) % NZ for n in shifts]
        size = R * len(planes)

        def columns_of(i, _):
            wide = pl.ds(pl.multiple_of(i * T, T), T)
            half[:size, wide] = jnp.dot(
                rows_by(lv, planes), step[:, wide], preferred_element_type=jnp.float32
            ).astype(jnp.bfloat16)
            return 0

        lax.fori_loop(0, B // T, columns_of, 0)

        def back(i, _):
            wide = pl.ds(pl.multiple_of(i * T, T), T)
            value = jnp.dot(half[:size], rt[:, wide], preferred_element_type=jnp.float32).astype(jnp.bfloat16)
            for n, zz in enumerate(planes):
                send3[zz, :, :, wide] = value[n * R : (n + 1) * R].reshape(NX, H, T)
            return 0

        lax.fori_loop(0, B // T, back, 0)

    for n in (4, 3, 2, 1):
        produce(*sorted({n, NZ - n}))
        for k in range(C):
            ring3.hop1(k, (n,))
    produce(0)
    for k in range(C):
        ring3.along_x(k)
        recv3[k][pl.ds(d, 1)] = send3[z, pl.ds(x, 1), :, cols(k)]

    def place(k):
        await_bytes(recv3[k].at[pl.ds(0, 31)], ring3.sf.at[k])

        def one(zz, _):
            for s in range(S):
                send4[k, zz, s] = recv3[k][owners[(s * NZ + zz) * NM + m]]
            return 0

        lax.fori_loop(0, NZ, one, 0)
        ring4.hop1(k)
        out[:, rows_of_plane(z), cols(k)] = send4[k, z]

    def finish(k):
        await_bytes(send4.at[k, pl.ds(0, 7)], ring4.sf.at[k])

    run((ring3.hop2, 0), (ring3.hop3, 0), (ring3.hop2, 1), (ring3.hop4, 0), (ring3.hop3, 1), (ring3.hop2, 2))
    run((place, 0), (ring3.hop4, 1), (ring3.hop3, 2), (ring3.hop2, 3), (place, 1), (ring3.hop4, 2), (ring3.hop3, 3))
    run((place, 2), (ring3.hop4, 3), (place, 3))
    for step_of in (ring4.hop2, ring4.hop3, ring4.hop4, finish):
        for k in range(C):
            step_of(k)

    for k in range(C):
        for ring in (ring1, ring2, ring3, ring4):
            ring.drain(k, recv1[k])
    await_bytes(part_z.at[pl.ds(0, NZ - 1)], pss.at[0])
    await_bytes(part_x.at[pl.ds(0, NX - 1)], pss.at[1])
    await_bytes(part_m.at[pl.ds(0, NM - 1)], pss.at[2])


def per_device(*args):
    bf16, f32 = jnp.bfloat16, jnp.float32
    whole = pl.BlockSpec(memory_space=pl.ANY)
    dma = pltpu.SemaphoreType.DMA

    def vmem(*shape):
        return pltpu.VMEM(shape, bf16)

    ring = [vmem(2, C, 10, H, W), vmem(2, C, 6, H, W), vmem(2, C, 2, H, W), dma((4, C)), dma((2, 3, C)), dma((max(C, 5),))]
    return pl.pallas_call(
        kernel,
        out_shape=vmem(S, Q, B),
        in_specs=[whole, pl.BlockSpec(memory_space=pltpu.SMEM), whole, whole, whole, whole],
        out_specs=pl.BlockSpec(memory_space=pltpu.VMEM),
        scratch_shapes=[
            vmem(S, Q, B),
            vmem(NZ, NX, H, B),
            vmem(B, B),
            vmem(B, B),
            vmem(B, B),
            vmem(B, B),
            vmem(B, B),
            vmem(C, ND, H, W),
            vmem(NZ, NX, H, B),
            vmem(3 * R, B),
            pltpu.VMEM((T, B), f32),
            pltpu.VMEM((T, B), f32),
            pltpu.VMEM((B, B), f32),
            vmem(B, B),
            vmem(NZ, NX, H, B),
            vmem(C, NZ, S, H, W),
            pltpu.SMEM((ND,), jnp.int32),
            pltpu.VMEM((3, 8, 128), f32),
            pltpu.VMEM((NZ, 8, 128), f32),
            pltpu.VMEM((NX, 8, 128), f32),
            pltpu.VMEM((NM, 8, 128), f32),
            dma((3,)),
            dma((3,)),
            dma((6,)),
        ]
        + [vmem(ND, H, W)] * (2 * C)
        + ring * 4,
        compiler_params=pltpu.CompilerParams(collective_id=0, has_side_effects=True, vmem_limit_bytes=58 << 20),
        cost_estimate=pl.CostEstimate(flops=8 * B**3, bytes_accessed=14 * B * B, transcendentals=2 * B * B),
        name="soap_step",
    )(*args)


def solution(mesh):
    placed = (
        P(None, "dp", "mp"),
        P(),
        P(("dp", "mp"), None, None),
        P(("dp", "mp"), None, None),
        P(("dp", "mp"), None, None),
        P(("dp", "mp"), None, None),
    )
    return jax.shard_map(
        per_device, mesh=mesh, in_specs=placed, out_specs=P(None, "dp", "mp"), check_vma=False
    )
```

```python
import math

import jax
import jax.numpy as jnp
from jax import lax
from jax.experimental import pallas as pl
from jax.experimental.pallas import tpu as pltpu
from jax.sharding import PartitionSpec as P

MESH = pl.DeviceIdType.MESH
B = 1024
S = 4
NZ, NX, NM = 8, 4, 8
ND = NZ * NX
Q = B // NX
H = Q // NZ
C = 4
W = B // C
T = 256
E = 16
R = NX * H

beta_one = 0.9
beta_two = 0.999
epsilon = 1e-08
correct_one = 1.0 - 0.9**3
correct_two = 1.0 - 0.999**3
clip_limit = 0.25 * math.sqrt(ND * NM * B * B)


def await_bytes(ref, sem):
    pltpu.make_async_copy(ref, ref, sem).wait()


def send(src, dst, send_sem, recv_sem, to):
    pltpu.make_async_remote_copy(
        src_ref=src, dst_ref=dst, send_sem=send_sem, recv_sem=recv_sem, device_id=to, device_id_type=MESH
    ).start()


class Ring:
    def __init__(self, source, deliver, spread, refs):
        self.source, self.deliver, self.spread = source, deliver, spread
        self.t1, self.t2, self.t3, self.ss, self.st, self.sf = refs
        d, self.m = lax.axis_index("dp"), lax.axis_index("mp")
        self.z, self.x = d // NX, d % NX

    def ways(self):
        for i, way in ((0, 1), (1, NZ - 1)):
            yield i, way, (((self.z + way) % NZ) * NX + self.x, self.m)

    def off(self, n):
        return (self.z + n) % NZ

    def land(self, piece, k, origin, way, hop, part):
        sem = self.sf.at[hop if self.spread == "hop" else k]
        zz = self.off(way)
        if not self.spread:
            send(piece(part), self.deliver(k, origin, part), self.ss.at[3, k], sem, (zz * NX + self.x, self.m))
            return
        for n in range(part.size):
            j = part.start + (self.x + n) % part.size
            send(piece(pl.ds(j, 1)), self.deliver(k, origin), self.ss.at[3, k], sem, (zz * NX + j, self.m))

    def hop1(self, k, planes=(4, 3, 2, 1), sides=(0, 1)):
        for i, way, to in self.ways():
            if i not in sides:
                continue
            for n, place in ((4, pl.ds(0, 2)), (3, pl.ds(2, 4)), (2, pl.ds(6, 4))):
                if n in planes:
                    zz, part = (self.off(4), pl.ds(2 * i, 2)) if n == 4 else (self.off(n * way), ALL)
                    send(self.source(k, zz, part), self.t1.at[i, k, place], self.ss.at[0, k], self.st.at[i, 0, k], to)
            if 1 in planes:
                self.land(lambda p: self.source(k, self.off(way), p), k, self.z, way, 1, ALL)

    def hop2(self, k):
        for i, way, to in self.ways():
            await_bytes(self.t1.at[i, k], self.st.at[i, 0, k])
            send(self.t1.at[i, k, pl.ds(0, 6)], self.t2.at[i, k], self.ss.at[1, k], self.st.at[i, 1, k], to)
            self.land(lambda p: self.t1.at[i, k, pl.ds(6 + p.start, p.size)], k, self.off(NZ - way), way, 2, ALL)

    def hop3(self, k):
        for i, way, to in self.ways():
            await_bytes(self.t2.at[i, k], self.st.at[i, 1, k])
            send(self.t2.at[i, k, pl.ds(0, 2)], self.t3.at[i, k], self.ss.at[2, k], self.st.at[i, 2, k], to)
            self.land(lambda p: self.t2.at[i, k, pl.ds(2 + p.start, p.size)], k, self.off(2 * (NZ - way)), way, 3, ALL)

    def hop4(self, k):
        for i, way, to in self.ways():
            await_bytes(self.t3.at[i, k], self.st.at[i, 2, k])
            self.land(
                lambda p: self.t3.at[i, k, pl.ds(p.start - 2 * i, p.size)],
                k, self.off(3 * (NZ - way)), way, 4, pl.ds(2 * i, 2))

    def along_x(self, k):
        for i in range(1, NX):
            xx = (self.x + i) % NX
            send(self.source(k, self.z, pl.ds(xx, 1)), self.deliver(k, self.z), self.ss.at[3, k],
                 self.sf.at[0 if self.spread == "hop" else k], (self.z * NX + xx, self.m))

    def drain(self, k, whole):
        await_bytes(self.t1.at[:, k], self.ss.at[0, k])
        await_bytes(self.t2.at[:, k], self.ss.at[1, k])
        await_bytes(self.t3.at[:, k], self.ss.at[2, k])
        await_bytes(whole.at[pl.ds(0, 31 if self.spread else 28)], self.ss.at[3, k])


ALL = pl.ds(0, 4)


def cols(k):
    return pl.ds(k * W, W)


def rows_of_plane(zz):
    return pl.ds(pl.multiple_of(zz * H, H), H)


def kernel(grad, owners, left, right, first, second, out,
           gbuf, lv, lt, rv, rt, m1v, m2v, send2, tile, half, rest0, rest1, turned, step, send3, send4,
           inverse, part, part_z, part_x, part_m, pss, psr, loc, *more):
    recv1, recv3, more = more[:C], more[C : 2 * C], more[2 * C :]
    rest = (rest0, rest1)
    d = lax.axis_index("dp")
    m = lax.axis_index("mp")
    z, x = d // NX, d % NX

    ring1 = Ring(
        lambda k, zz, part: gbuf.at[part, rows_of_plane(zz), cols(k)],
        lambda k, zz, part: recv1[k].at[pl.ds(zz * S + part.start, part.size)],
        None, more[0:6])
    ring2 = Ring(
        lambda k, zz, part: send2.at[k, pl.ds(zz * NX + part.start, part.size)],
        lambda k, zz: tile.at[zz, pl.ds(x, 1), :, cols(k)],
        "hop", more[6:12])
    ring3 = Ring(
        lambda k, zz, part: send3.at[zz, part, :, cols(k)],
        lambda k, zz: recv3[k].at[pl.ds(zz * NX + x, 1)],
        "chunk", more[12:18])
    ring4 = Ring(
        lambda k, zz, part: send4.at[k, zz, part],
        lambda k, zz, part: out.at[part, rows_of_plane(zz), cols(k)],
        None, more[18:24])

    barrier = pltpu.get_barrier_semaphore()

    def along_z(i):
        return (((z + i) % NZ) * NX + x, m)

    def along_x(i):
        return (z * NX + (x + i) % NX, m)

    def along_m(i):
        return (d, (m + i) % NM)

    local = [
        pltpu.make_async_copy(grad, gbuf, loc.at[0]),
        pltpu.make_async_copy(right.at[0], rv, loc.at[2]),
        pltpu.make_async_copy(first.at[0], m1v, loc.at[3]),
        pltpu.make_async_copy(second.at[0], m2v, loc.at[4]),
    ]
    local[0].start()

    met = [along_z(i) for i in range(1, NZ)] + [along_x(i) for i in range(1, NX)] + [along_m(i) for i in range(1, NM)]
    met += [(((z + way) % NZ) * NX + (x + i) % NX, m) for way in (1, NZ - 1) for i in range(1, NX)]
    for other in met:
        pl.semaphore_signal(barrier, inc=1, device_id=other, device_id_type=MESH)
    local[0].wait()
    pl.semaphore_wait(barrier, len(met))

    def gather_sum(n, value, held, place, axis, size):
        part[n] = value
        held[place] = value
        for i in range(1, size):
            send(part.at[n], held.at[place], pss.at[n], psr.at[n], axis(i))

    def sum_of(n, held, size):
        await_bytes(held.at[pl.ds(0, size - 1)], psr.at[n])
        total = held[0]
        for i in range(1, size):
            total = total + held[i]
        return total

    def squares():
        def add(i, acc):
            block = gbuf[i // 16, pl.ds(pl.multiple_of((i % 16) * 16, 16), 16), :].astype(jnp.float32)
            return acc + block * block

        acc = lax.fori_loop(0, 64, add, jnp.zeros((16, B), jnp.float32))
        acc = acc[:8] + acc[8:]
        total = acc[:, :128]
        for i in range(1, 8):
            total = total + acc[:, i * 128 : (i + 1) * 128]
        gather_sum(0, total, part_z, z, along_z, NZ)

    def invert(low, high):
        def one(o, _):
            found = jnp.int32(0)
            for j in range(ND):
                found = found + jnp.where(owners[j * NM + m] == o, (j % NZ) * S + j // NZ, 0)
            inverse[o] = jnp.minimum(found, ND - 1)
            return 0

        lax.fori_loop(low, high, one, 0)

    def fetch():
        def one(i, _):
            rows = pl.ds(pl.multiple_of((i % NX) * Q + (i // NX) * H, H), H)
            pltpu.make_async_copy(left.at[0, rows, :], lv.at[i // NX, i % NX], loc.at[1]).start()
            return 0

        lax.fori_loop(0, ND, one, 0)
        for copy in local[1:]:
            copy.start()

    def lanes(zz):
        return pl.ds(pl.multiple_of(zz * R, R), R)

    def turn():
        await_bytes(lv, loc.at[1])

        def one(zz, _):
            lt[:, lanes(zz)] = lv[zz].reshape(R, B).T
            return 0

        lax.fori_loop(0, NZ, one, 0)

    def pack(k):
        for s in range(S):
            recv1[k][z * S + s] = gbuf[s, rows_of_plane(z), cols(k)]
        await_bytes(recv1[k].at[pl.ds(0, 28)], ring1.sf.at[k])

        def one(o, _):
            send2[k, o] = recv1[k][inverse[o]]
            return 0

        lax.fori_loop(0, ND, one, 0, unroll=4)

    def rows_by(ref, planes):
        return jnp.concatenate([ref[zz].reshape(R, B) for zz in planes], axis=0)

    def rotate_rows(at, *shifts):
        planes = [(z + n) % NZ for n in shifts]
        size = R * len(planes)

        def columns_of(i, _):
            wide = pl.ds(pl.multiple_of(i * T, T), T)
            half[at : at + size, wide] = jnp.dot(
                rows_by(tile, planes), rv[:, wide], preferred_element_type=jnp.float32
            ).astype(jnp.bfloat16)
            return 0

        lax.fori_loop(0, B // T, columns_of, 0)

    def left_rows(rows, *shifts):
        basis = jnp.concatenate([lt[rows, lanes((z + n) % NZ)] for n in shifts], axis=1)
        return jnp.dot(basis, half[: R * len(shifts)], preferred_element_type=jnp.float32)

    def rotate(*shifts):
        rotate_rows(0, *shifts)

        def rows_of(i, _):
            rows = pl.ds(pl.multiple_of(i * T, T), T)
            if shifts == (0,):
                turned[rows, :] = left_rows(rows, *shifts)
            else:
                turned[rows, :] += left_rows(rows, *shifts)
            return 0

        lax.fori_loop(0, B // T, rows_of, 0)

    for k in range(C):
        ring1.hop1(k)
    squares()
    fetch()

    def onward(k):
        pack(k)
        ring2.hop1(k)
        ring2.along_x(k)
        tile[z, pl.ds(x, 1), :, cols(k)] = send2[k, pl.ds(d, 1)]

    def run(*steps):
        for step_of, k in steps:
            step_of(k)

    ring1.hop2(0)
    invert(0, ND // 2)
    run((ring1.hop3, 0), (ring1.hop2, 1))
    invert(ND // 2, ND)
    run((ring1.hop4, 0), (ring1.hop3, 1), (ring1.hop2, 2))
    turn()
    run((onward, 0), (ring1.hop4, 1), (ring1.hop3, 2), (ring1.hop2, 3))
    run((onward, 1), (ring1.hop4, 2), (ring1.hop3, 3), (onward, 2), (ring1.hop4, 3), (onward, 3))
    gather_sum(1, sum_of(0, part_z, NZ), part_x, x, along_x, NX)
    for k in range(C):
        ring2.hop2(k)
    local[1].wait()
    await_bytes(tile.at[0, pl.ds(0, NX - 1)], ring2.sf.at[0])
    rotate(0)

    def turn_right(i, _):
        rows = pl.ds(pl.multiple_of(i * T, T), T)
        rt[:, rows] = rv[rows, :].T
        return 0

    lax.fori_loop(0, B // T, turn_right, 0)
    gather_sum(2, sum_of(1, part_x, NX), part_m, m, along_m, NM)
    for k in range(C):
        ring2.hop3(k)
    await_bytes(tile.at[pl.ds(0, 2)], ring2.sf.at[1])
    rotate(1, 7)
    for k in range(C):
        ring2.hop4(k)
    await_bytes(tile.at[pl.ds(0, 2)], ring2.sf.at[2])
    rotate(2, 6)
    await_bytes(tile.at[pl.ds(0, 2)], ring2.sf.at[3])
    rotate_rows(0, 3, 5)
    await_bytes(tile.at[0], ring2.sf.at[4])
    rotate_rows(2 * R, 4)

    total_squares = jnp.sum(sum_of(2, part_m, NM), keepdims=True)
    factor = jnp.minimum(jnp.float32(1.0), clip_limit / jnp.sqrt(total_squares))
    local[2].wait()
    local[3].wait()

    def precondition(i):
        more = rest[i % 2]
        more[...] = left_rows(pl.ds(i * T, T), 3, 5, 4)
        for n in range(0, T, E):
            rows = pl.ds(i * T + n, E)
            t = (turned[rows, :] + more[n : n + E, :]) * factor
            first_new = (beta_one / correct_one) * m1v[rows, :].astype(jnp.float32)
            first_new = first_new + ((1.0 - beta_one) / correct_one) * t
            second_new = (beta_two / correct_two) * m2v[rows, :].astype(jnp.float32)
            second_new = second_new + ((1.0 - beta_two) / correct_two) * (t * t)
            value = first_new / (second_new * lax.rsqrt(second_new) + epsilon)
            step[rows, :] = value.astype(jnp.bfloat16)

    for i in range(B // T):
        precondition(i)

    def produce(*shifts):
        planes = [(z + n) % NZ for n in shifts]
        size = R * len(planes)

        def columns_of(i, _):
            wide = pl.ds(pl.multiple_of(i * T, T), T)
            half[:size, wide] = jnp.dot(
                rows_by(lv, planes), step[:, wide], preferred_element_type=jnp.float32
            ).astype(jnp.bfloat16)
            return 0

        lax.fori_loop(0, B // T, columns_of, 0)

        def back(i, _):
            wide = pl.ds(pl.multiple_of(i * T, T), T)
            value = jnp.dot(half[:size], rt[:, wide], preferred_element_type=jnp.float32).astype(jnp.bfloat16)
            for n, zz in enumerate(planes):
                send3[zz, :, :, wide] = value[n * R : (n + 1) * R].reshape(NX, H, T)
            return 0

        lax.fori_loop(0, B // T, back, 0)

    produce(4)
    for k in range(C):
        ring3.hop1(k, (4,))
    for n in (3, 2, 1):
        for side, shift in enumerate((n, NZ - n)):
            produce(shift)
            for k in range(C):
                ring3.hop1(k, (n,), (side,))
    produce(0)
    for k in range(C):
        ring3.along_x(k)
        recv3[k][pl.ds(d, 1)] = send3[z, pl.ds(x, 1), :, cols(k)]

    def place(k):
        await_bytes(recv3[k].at[pl.ds(0, 31)], ring3.sf.at[k])

        def one(zz, _):
            for s in range(S):
                send4[k, zz, s] = recv3[k][owners[(s * NZ + zz) * NM + m]]
            return 0

        lax.fori_loop(0, NZ, one, 0)
        ring4.hop1(k)
        out[:, rows_of_plane(z), cols(k)] = send4[k, z]

    def finish(k):
        await_bytes(send4.at[k, pl.ds(0, 7)], ring4.sf.at[k])

    run((ring3.hop2, 0), (ring3.hop3, 0), (ring3.hop2, 1), (ring3.hop4, 0), (ring3.hop3, 1), (ring3.hop2, 2))
    run((place, 0), (ring3.hop4, 1), (ring3.hop3, 2), (ring3.hop2, 3), (place, 1), (ring3.hop4, 2), (ring3.hop3, 3))
    run((place, 2), (ring3.hop4, 3), (place, 3))
    for step_of in (ring4.hop2, ring4.hop3, ring4.hop4, finish):
        for k in range(C):
            step_of(k)

    for k in range(C):
        for ring in (ring1, ring2, ring3, ring4):
            ring.drain(k, recv1[k])
    await_bytes(part_z.at[pl.ds(0, NZ - 1)], pss.at[0])
    await_bytes(part_x.at[pl.ds(0, NX - 1)], pss.at[1])
    await_bytes(part_m.at[pl.ds(0, NM - 1)], pss.at[2])


def per_device(*args):
    bf16, f32 = jnp.bfloat16, jnp.float32
    whole = pl.BlockSpec(memory_space=pl.ANY)
    dma = pltpu.SemaphoreType.DMA

    def vmem(*shape):
        return pltpu.VMEM(shape, bf16)

    ring = [vmem(2, C, 10, H, W), vmem(2, C, 6, H, W), vmem(2, C, 2, H, W), dma((4, C)), dma((2, 3, C)), dma((max(C, 5),))]
    return pl.pallas_call(
        kernel,
        out_shape=vmem(S, Q, B),
        in_specs=[whole, pl.BlockSpec(memory_space=pltpu.SMEM), whole, whole, whole, whole],
        out_specs=pl.BlockSpec(memory_space=pltpu.VMEM),
        scratch_shapes=[
            vmem(S, Q, B),
            vmem(NZ, NX, H, B),
            vmem(B, B),
            vmem(B, B),
            vmem(B, B),
            vmem(B, B),
            vmem(B, B),
            vmem(C, ND, H, W),
            vmem(NZ, NX, H, B),
            vmem(3 * R, B),
            pltpu.VMEM((T, B), f32),
            pltpu.VMEM((T, B), f32),
            pltpu.VMEM((B, B), f32),
            vmem(B, B),
            vmem(NZ, NX, H, B),
            vmem(C, NZ, S, H, W),
            pltpu.SMEM((ND,), jnp.int32),
            pltpu.VMEM((3, 8, 128), f32),
            pltpu.VMEM((NZ, 8, 128), f32),
            pltpu.VMEM((NX, 8, 128), f32),
            pltpu.VMEM((NM, 8, 128), f32),
            dma((3,)),
            dma((3,)),
            dma((6,)),
        ]
        + [vmem(ND, H, W)] * (2 * C)
        + ring * 4,
        compiler_params=pltpu.CompilerParams(collective_id=0, has_side_effects=True, vmem_limit_bytes=58 << 20),
        cost_estimate=pl.CostEstimate(flops=8 * B**3, bytes_accessed=14 * B * B, transcendentals=2 * B * B),
        name="soap_step",
    )(*args)


def solution(mesh):
    placed = (
        P(None, "dp", "mp"),
        P(),
        P(("dp", "mp"), None, None),
        P(("dp", "mp"), None, None),
        P(("dp", "mp"), None, None),
        P(("dp", "mp"), None, None),
    )
    return jax.shard_map(
        per_device, mesh=mesh, in_specs=placed, out_specs=P(None, "dp", "mp"), check_vma=False
    )
```
